768 devices in a mesh: blk: 32 (over z_lo, x, core), cap: 24 (over z_hi, y).
Axes of the slice: x: 4, y: 8, z: 12 (z_hi: 3, z_lo: 4; z = z_hi * 4 + z_lo), core: 2. Of those that a mesh axis runs over, the one named last changes fastest.
Arguments:
- image_emb: bfloat16 [36864, 1152], P(('blk', 'cap')), may hold values from -0.4375 to 0.4375
- text_emb: bfloat16 [36864, 1152], P(('blk', 'cap')), may hold values from -0.4375 to 0.4375
- caption_emb: bfloat16 [294912, 1152], P(('blk', 'cap')), may hold values from -0.4375 to 0.4375
- logit_scale: float32 [1], replicated, may hold values from 8 to 32
- logit_bias: float32 [1], replicated, may hold values from -4 to -2
- caption_owner: int32 [294912], P(('blk', 'cap')), may hold values from 0 to 47, as said below
- caption_valid: int32 [294912], P(('blk', 'cap')), may hold values from 0 to 1, as said below
- caption_count: int32 [36864], P(('blk', 'cap')), may hold values from 0 to 8, as said below
Outputs:
- row_loss: float32 [36864], P(('blk', 'cap'))
- image_grad: float32 [36864, 1152], P(('blk', 'cap'))
- text_grad: float32 [36864, 1152], P(('blk', 'cap'))
- caption_grad: bfloat16 [294912, 1152], P(('blk', 'cap'))
The draws below stay inside these ranges and needn't reach their ends.
Inputs may be any that keep to these rules, and one draw needn't show every extreme that they name: `caption_owner`: each image owns exactly 8 of the 384 slots arriving at its device; every local row is an owner. `caption_valid`: an image's valid slots number exactly its caption_count. `caption_count`: every device holds an image with 8 extra captions.
All inputs are finite; a program needn't handle non-finite values.
Results may differ from the reference program's by a relative error of at most 0.011.
Values may be sent and summed in bfloat16 or wider, within the bound.
No kernel may reach another device: no remote copies, remote signals or barrier semaphores. Data moves between devices by JAX's collectives and lax.ppermute only.
A program may use at most 32 MiB of HBM per device.

```python
import math
import jax
import jax.numpy as jnp
from jax import lax

D = 1152
I_DEV = 48
TEXTS = 1536
IMAGES = 36864
CAP_DEV = 384
SLOT = 16
N_BLK = 32
N_CAP = 24


def slot_tables(key):
    devices = N_BLK * N_CAP
    keys = jax.random.split(key, devices)
    perms = jax.vmap(lambda one: jax.random.permutation(one, CAP_DEV))(keys).astype(jnp.int32)
    counts = jax.random.randint(jax.random.fold_in(key, 101), (devices, I_DEV), 0, 9).astype(jnp.int32)
    chosen = jax.random.randint(jax.random.fold_in(key, 102), (devices, 1), 0, I_DEV).astype(jnp.int32)
    counts = jnp.where(jnp.arange(I_DEV, dtype=jnp.int32)[None, :] == chosen, 8, counts).astype(jnp.int32)
    owner = (perms // 8).astype(jnp.int32)
    rank = (perms % 8).astype(jnp.int32)
    valid = (rank < jnp.take_along_axis(counts, owner, axis=1)).astype(jnp.int32)
    return (owner, valid, counts)


def draw_caption_owner(key, part):
    owner, valid, counts = slot_tables(key)
    return owner.reshape(-1)


def draw_caption_valid(key, part):
    owner, valid, counts = slot_tables(key)
    return valid.reshape(-1)


def draw_caption_count(key, part):
    owner, valid, counts = slot_tables(key)
    return counts.reshape(-1)


def levels(own_key, dims, cuts, smallest, largest):
    loudness = 1.0
    for position, blocks in cuts:
        steps = jax.random.uniform(jax.random.fold_in(jax.random.fold_in(own_key, 6), position), (blocks,), jnp.float32, smallest / len(cuts), largest / len(cuts))
        loudness = loudness * jnp.repeat(jnp.exp(steps), dims[position] // blocks).reshape((-1,) + (1,) * (len(dims) - 1 - position))
    return loudness


def scatter_about(key, dims, scale, reach, cuts=(), kind=jnp.bfloat16):
    drawn = scale * jax.random.normal(key, dims, jnp.float32)
    if cuts:
        drawn = drawn * levels(key, dims, cuts, -0.22, 0.18)
    return jnp.clip(drawn, -reach, reach).astype(kind)


def setup_inputs(seed: int = 0) -> dict:
    arg_keys = jax.random.split(jax.random.key(seed), 9)
    return {
        "image_emb": scatter_about(arg_keys[0], (IMAGES, D), (D ** -0.5), 0.4375, ((0, 768),)),
        "text_emb": scatter_about(arg_keys[1], (IMAGES, D), (D ** -0.5), 0.4375, ((0, 768),)),
        "caption_emb": scatter_about(arg_keys[2], (N_BLK * N_CAP * CAP_DEV, D), (D ** -0.5), 0.4375, ((0, 768),)),
        "logit_scale": jnp.clip(jnp.exp(jax.random.uniform(arg_keys[3], (1,), jnp.float32, math.log(8.0), math.log(32.0))), 8.0, 32.0),
        "logit_bias": jnp.clip(jax.random.uniform(arg_keys[4], (1,), jnp.float32, -4.0, -2.0), -4.0, -2.0),
        "caption_owner": draw_caption_owner(jax.random.fold_in(arg_keys[8], 71), 0),
        "caption_valid": draw_caption_valid(jax.random.fold_in(arg_keys[8], 71), 0),
        "caption_count": draw_caption_count(jax.random.fold_in(arg_keys[8], 71), 0),
    }


def group_terms(pair, scale, bias):
    images, texts = pair
    logits = scale * jnp.dot(images, texts.T, preferred_element_type=jnp.float32) + bias
    rows = lax.broadcasted_iota(jnp.int32, logits.shape, 0)
    cols = lax.broadcasted_iota(jnp.int32, logits.shape, 1)
    signs = jnp.where(rows == cols, jnp.float32(1.0), jnp.float32(-1.0))
    losses = jnp.sum(jax.nn.softplus(-signs * logits), axis=1)
    coeff = (-signs * jax.nn.sigmoid(-signs * logits)).astype(jnp.bfloat16)
    image_part = jnp.dot(coeff, texts, preferred_element_type=jnp.float32)
    text_sum = jnp.dot(coeff.T, images, preferred_element_type=jnp.float32)
    return losses, image_part, scale * text_sum


def caption_terms(images, arrived, owner, valid, count, scale, bias):
    picked = images[owner].astype(jnp.float32)
    cap_logit = scale * jnp.sum(picked * arrived.astype(jnp.float32), axis=1) + bias
    denom = jnp.maximum(count[owner], 1).astype(jnp.float32)
    flags = valid.astype(jnp.float32)
    cap_loss = flags * jax.nn.softplus(-cap_logit) / denom
    cap_coeff = (flags * (jax.nn.sigmoid(cap_logit) - 1.0) / denom).astype(jnp.bfloat16)
    select = (owner[:, None] == jnp.arange(images.shape[0], dtype=jnp.int32)[None, :]).astype(jnp.float32)
    extra = jnp.dot(cap_loss, select)
    weights = (select * cap_coeff.astype(jnp.float32)[:, None]).astype(jnp.bfloat16)
    cap_part = jnp.dot(weights.T, arrived, preferred_element_type=jnp.float32)
    cap_grad = (scale * cap_coeff.astype(jnp.float32)[:, None] * picked).astype(jnp.bfloat16)
    return extra, cap_part, cap_grad


def reference(image_emb, text_emb, caption_emb, logit_scale, logit_bias, caption_owner, caption_valid, caption_count):
    scale = logit_scale[0]
    bias = logit_bias[0]
    image_groups = image_emb.reshape(N_BLK, N_CAP, I_DEV, D).transpose(1, 0, 2, 3).reshape(N_CAP, TEXTS, D)
    text_groups = text_emb.reshape(N_BLK, N_CAP, I_DEV, D).transpose(1, 0, 2, 3).reshape(N_CAP, TEXTS, D)
    losses, image_part, text_grad = lax.map(lambda pair: group_terms(pair, scale, bias), (image_groups, text_groups))

    def back(array):
        tail = array.shape[2:]
        moved = array.reshape((N_CAP, N_BLK, I_DEV) + tail)
        order = (1, 0, 2) + tuple(range(3, 3 + len(tail)))
        return moved.transpose(order).reshape((N_BLK * N_CAP, I_DEV) + tail)

    losses = back(losses)
    image_part = back(image_part)
    text_grad = back(text_grad)

    arrived = caption_emb.reshape(N_BLK, N_CAP, N_CAP, SLOT, D).transpose(0, 2, 1, 3, 4).reshape(N_BLK * N_CAP, CAP_DEV, D)
    owner = caption_owner.reshape(N_BLK * N_CAP, CAP_DEV)
    valid = caption_valid.reshape(N_BLK * N_CAP, CAP_DEV)
    count = caption_count.reshape(N_BLK * N_CAP, I_DEV)
    images = image_emb.reshape(N_BLK * N_CAP, I_DEV, D)
    extra, cap_part, cap_grad = jax.vmap(lambda a, b2, c, d, e: caption_terms(a, b2, c, d, e, scale, bias))(images, arrived, owner, valid, count)

    row_loss = (losses + extra).reshape(IMAGES)
    image_grad = (scale * (image_part + cap_part)).reshape(IMAGES, D)
    caption_grad = cap_grad.reshape(N_BLK, N_CAP, N_CAP, SLOT, D).transpose(0, 2, 1, 3, 4).reshape(N_BLK * N_CAP * CAP_DEV, D)
    return row_loss, image_grad, text_grad.reshape(IMAGES, D), caption_grad
```

```python
import jax
import jax.numpy as jnp
from jax import lax
from jax.sharding import PartitionSpec as P

N_ZL, N_X, N_C = 4, 4, 2
N_ZH, N_Y = 3, 8
LANES = 128


def blk_of(zl, x, c):
    return (zl * N_X + x) * N_C + c


def shift_zl(k):
    return [
        (blk_of(z, x, c), blk_of((z + k) % N_ZL, x, c))
        for z in range(N_ZL) for x in range(N_X) for c in range(N_C)
    ]


def shift_x(k):
    return [
        (blk_of(z, x, c), blk_of(z, (x + k) % N_X, c))
        for z in range(N_ZL) for x in range(N_X) for c in range(N_C)
    ]


def swap_c():
    return [
        (blk_of(z, x, c), blk_of(z, x, 1 - c))
        for z in range(N_ZL) for x in range(N_X) for c in range(N_C)
    ]


def shift_zh(k):
    return [(h * N_Y + y, ((h + k) % N_ZH) * N_Y + y) for h in range(N_ZH) for y in range(N_Y)]


Y_GROUPS = [[h * N_Y + y for y in range(N_Y)] for h in range(N_ZH)]


def shards(image, text, caption, logit_scale, logit_bias, owner, valid, count):
    f32, bf16 = jnp.float32, jnp.bfloat16
    scale = logit_scale[0]
    bias = logit_bias[0]
    rows, width = image.shape
    slots = caption.shape[0]
    run = slots // (N_ZH * N_Y)
    third = slots // N_ZH
    zh = lax.axis_index("cap") // N_Y

    runs = caption.reshape(N_ZH, N_Y, run, width)
    order = [lax.rem(zh + (N_ZH - k), N_ZH) for k in range(N_ZH)]
    outgoing = jnp.stack([lax.dynamic_index_in_dim(runs, o, 0, False) for o in order], axis=1)
    arrived = lax.all_to_all(
        outgoing.reshape(N_Y, N_ZH * run, width), "cap", 0, 0, axis_index_groups=Y_GROUPS, tiled=True
    )
    arrived = arrived.reshape(N_Y, N_ZH, run, width)

    number = jnp.maximum(count, 1)
    holds = owner[None, :] == jnp.arange(rows, dtype=jnp.int32)[:, None]
    marks = jnp.where(holds & (valid[None, :] > 0), number[:, None], 0).astype(bf16)

    def with_marks(k):
        to = lax.rem(zh + k, N_ZH)
        part = lax.dynamic_slice_in_dim(marks, to * third, third, 1)
        return jnp.concatenate([image, part], axis=1)

    tagged = [with_marks(k) for k in range(N_ZH)]
    tagged = [tagged[0]] + [lax.ppermute(tagged[k], "cap", shift_zh(k)) for k in range(1, N_ZH)]

    texts = [text] + [lax.ppermute(text, "blk", shift_zl(k)) for k in range(1, N_ZL)]
    texts = jnp.concatenate(texts, axis=0)
    images = [image] + [lax.ppermute(image, "blk", shift_x(k)) for k in range(1, N_X)]
    images = jnp.concatenate(images, axis=0)
    images = jnp.concatenate([images, lax.ppermute(images, "blk", swap_c())], axis=0)

    logits = scale * jnp.dot(images, texts.T, preferred_element_type=f32) + bias
    left = lax.broadcasted_iota(jnp.int32, logits.shape, 0)
    right = lax.broadcasted_iota(jnp.int32, logits.shape, 1)
    signs = jnp.where((left == right) & (left < rows), f32(1.0), f32(-1.0))
    losses = jnp.sum(jax.nn.softplus(-signs * logits), axis=1)
    coeff = (-signs * jax.nn.sigmoid(-signs * logits)).astype(bf16)
    image_part = jnp.dot(coeff, texts, preferred_element_type=f32)
    text_part = jnp.dot(coeff.T, images, preferred_element_type=f32)

    def tag(grad, loss):
        high = loss.astype(bf16)
        low = (loss - high.astype(f32)).astype(bf16)
        lane = lax.broadcasted_iota(jnp.int32, (loss.shape[0], LANES), 1)
        extra = jnp.where(lane == 0, high[:, None], jnp.where(lane == 1, low[:, None], 0).astype(bf16))
        return jnp.concatenate([grad.astype(bf16), extra], axis=1)

    half = rows * N_X
    sent = tag(image_part, losses)
    got = lax.ppermute(sent[half:], "blk", swap_c()).astype(f32)
    grad_x = image_part[:half] + got[:, :width]
    loss_x = losses[:half] + got[:, width] + got[:, width + 1]
    sent = tag(grad_x, loss_x)
    image_sum = grad_x[:rows]
    loss_sum = loss_x[:rows]
    for k in range(1, N_X):
        back = lax.ppermute(sent[k * rows:(k + 1) * rows], "blk", shift_x(-k)).astype(f32)
        image_sum += back[:, :width]
        loss_sum += back[:, width] + back[:, width + 1]
    text_sum = text_part[:rows]
    for k in range(1, N_ZL):
        part = text_part[k * rows:(k + 1) * rows].astype(bf16)
        text_sum += lax.ppermute(part, "blk", shift_zl(-k)).astype(f32)

    cap_grads = []
    for k in range(N_ZH):
        e = arrived[:, k].reshape(third, width)
        i = tagged[k][:, :width]
        mark = tagged[k][:, width:].astype(f32)
        logit = scale * jnp.dot(i, e.T, preferred_element_type=f32) + bias
        there = mark > 0
        denom = jnp.where(there, mark, f32(1.0))
        loss = jnp.sum(jnp.where(there, jax.nn.softplus(-logit) / denom, 0.0), axis=1)
        weight = jnp.where(there, (jax.nn.sigmoid(logit) - 1.0) / denom, 0.0).astype(bf16)
        part = jnp.dot(weight, e, preferred_element_type=f32)
        cap_grads.append((scale * jnp.dot(weight.T, i, preferred_element_type=f32)).astype(bf16))
        if k == 0:
            image_sum += part
            loss_sum += loss
        else:
            back = lax.ppermute(tag(part, loss), "cap", shift_zh(-k)).astype(f32)
            image_sum += back[:, :width]
            loss_sum += back[:, width] + back[:, width + 1]
    back = jnp.stack([g.reshape(N_Y, run, width) for g in cap_grads], axis=1)
    back = lax.all_to_all(
        back.reshape(N_Y, N_ZH * run, width), "cap", 0, 0, axis_index_groups=Y_GROUPS, tiled=True
    )
    back = back.reshape(N_Y, N_ZH, run, width)
    place = [lax.rem(zh + (N_ZH - h), N_ZH) for h in range(N_ZH)]
    caption_grad = jnp.stack([lax.dynamic_index_in_dim(back, o, 1, False) for o in place], axis=0)
    return loss_sum, scale * image_sum, scale * text_sum, caption_grad.reshape(slots, width)


def solution(mesh):
    both = ("blk", "cap")
    in_specs = (P(both, None), P(both, None), P(both, None), P(), P(), P(both), P(both), P(both))
    out_specs = (P(both), P(both, None), P(both, None), P(both, None))
    return jax.shard_map(shards, mesh=mesh, in_specs=in_specs, out_specs=out_specs, check_vma=False)
```

```python
import jax
import jax.numpy as jnp
from jax import lax
from jax.experimental import pallas as pl
from jax.experimental.pallas import tpu as pltpu
from jax.sharding import PartitionSpec as P

N_ZL, N_X, N_C = 4, 4, 2
N_ZH, N_Y = 3, 8
LANES = 128
LATE = 200_000_000_000
PREP, JOIN, STACK, CAPS, FOLD, FOLD2 = 0, LATE, 5_000_000_000, LATE, LATE, 0

F32, BF16 = jnp.float32, jnp.bfloat16
SMEM = pl.BlockSpec(memory_space=pltpu.SMEM)
VMEM = pl.BlockSpec(memory_space=pltpu.VMEM)
ANY = pl.BlockSpec(memory_space=pl.ANY)
HBM = pl.BlockSpec(memory_space=pltpu.HBM)


def partners(zl_bits, x_bits, c_bits):
    def blk_of(zl, x, c):
        return (zl * N_X + x) * N_C + c

    return [
        (blk_of(z, x, c), blk_of(z ^ zl_bits, x ^ x_bits, c ^ c_bits))
        for z in range(N_ZL) for x in range(N_X) for c in range(N_C)
    ]


ZL_NEAR, ZL_FAR = partners(1, 0, 0), partners(2, 0, 0)
X_NEAR, X_FAR = partners(0, 1, 0), partners(0, 3, 0)
OTHER_CORE = partners(0, 0, 1)
Y_GROUPS = [[h * N_Y + y for y in range(N_Y)] for h in range(N_ZH)]


def shift_zh(k):
    return [(h * N_Y + y, ((h + k) % N_ZH) * N_Y + y) for h in range(N_ZH) for y in range(N_Y)]


def call(body, outs, ins, in_specs, out_specs=None, scratch=(), flops=0, moved=0, room=8):
    return pl.pallas_call(
        body,
        out_shape=tuple(jax.ShapeDtypeStruct(s, d) for s, d in outs),
        in_specs=in_specs,
        out_specs=tuple(out_specs or [VMEM] * len(outs)),
        scratch_shapes=list(scratch),
        cost_estimate=pl.CostEstimate(flops=flops, bytes_accessed=moved, transcendentals=0),
        compiler_params=pltpu.CompilerParams(vmem_limit_bytes=room * 1024 * 1024),
    )(*ins)


def nt(a, b):
    return lax.dot_general(a, b, (((1,), (1,)), ((), ())), preferred_element_type=F32)


def tn(a, b):
    return lax.dot_general(a, b, (((0,), (0,)), ((), ())), preferred_element_type=F32)


def nn(a, b):
    return jnp.dot(a, b, preferred_element_type=F32)


def soft_terms(u):
    e = jnp.exp(-jnp.abs(u))
    return jnp.maximum(u, 0.0) + jnp.log1p(e), jnp.where(u >= 0, 1.0, e) / (1.0 + e)


def loss_lanes(loss):
    lane = lax.broadcasted_iota(jnp.int32, (loss.shape[0], LANES), 1)
    return jnp.where(lane == 0, loss, 0.0)


def split_lanes(extra):
    lane = lax.broadcasted_iota(jnp.int32, extra.shape, 1)
    value = jnp.sum(jnp.where(lane == 0, extra, 0.0), axis=1, keepdims=True)
    high = value.astype(BF16).astype(F32)
    return jnp.where(lane == 0, high, jnp.where(lane == 1, value - high, 0.0)).astype(BF16)


def join_lanes(extra):
    lane = lax.broadcasted_iota(jnp.int32, extra.shape, 1)
    return jnp.where(lane == 0, jnp.sum(extra, axis=1, keepdims=True), 0.0)


def prepare(zh_ref, caption, image, owner, valid, count, outgoing, tag1, tag2, own_marks,
            image_v, owner_v, valid_v, count_v, sems, more_sems):
    zh = zh_ref[0]
    rows, width = image.shape
    third = owner.shape[1] // N_ZH
    small = [
        pltpu.make_async_copy(src, dst, more_sems.at[n])
        for n, (src, dst) in enumerate(((owner, owner_v), (valid, valid_v), (count, count_v), (image, image_v)))
    ]
    copies = [
        pltpu.make_async_copy(caption.at[lax.rem(zh + (N_ZH - k), N_ZH)], outgoing.at[:, k], sems.at[k])
        for k in range(N_ZH)
    ]
    for copy in small + copies:
        copy.start()
    for copy in small:
        copy.wait()
    diagonal = lax.broadcasted_iota(jnp.int32, (rows, rows), 0) == lax.broadcasted_iota(jnp.int32, (rows, rows), 1)
    number = jnp.sum(jnp.where(diagonal, count_v[...].astype(F32), 0.0), axis=1, keepdims=True)
    number = jnp.maximum(number, 1.0)
    holds = owner_v[...] == lax.broadcasted_iota(jnp.int32, (rows, N_ZH * third), 0)
    marks = jnp.where(holds & (valid_v[...] > 0), number, 0.0).astype(BF16)
    parts = [marks[:, h * third:(h + 1) * third] for h in range(N_ZH)]
    for k, ref in enumerate((own_marks, tag1, tag2)):
        to = lax.rem(zh + k, N_ZH)
        part = jnp.where(to == 0, parts[0], jnp.where(to == 1, parts[1], parts[2]))
        if k == 0:
            ref[...] = part
        else:
            ref[:, :width] = image_v[...]
            ref[:, width:] = part
    for copy in copies:
        copy.wait()


def join(image, got_image, text, got_text, after, images, texts):
    for first, second, out in ((image, got_image, images), (text, got_text, texts)):
        rows = first.shape[0]
        out[:rows, :] = first[...]
        out[rows:, :] = second[...]


def stack(images1, images2, texts1, texts2, images, texts):
    for first, second, out in ((images1, images2, images), (texts1, texts2, texts)):
        rows = first.shape[0]
        out[:rows, :] = first[...]
        out[rows:, :] = second[...]


def pairs(scale_ref, bias_ref, near_images, far_images, texts, keep, send, keep_text, send_text, rows):
    width = texts.shape[1]
    half = texts.shape[0] // 2
    sums = None
    for images in (near_images, far_images):
        logits = scale_ref[0] * nt(images[...], texts[...]) + bias_ref[0]
        if images is near_images:
            left = lax.broadcasted_iota(jnp.int32, logits.shape, 0)
            right = lax.broadcasted_iota(jnp.int32, logits.shape, 1)
            match = (left == right) & (left < rows)
            loss, slope = soft_terms(jnp.where(match, -logits, logits))
            coeff = jnp.where(match, -slope, slope).astype(BF16)
        else:
            loss, slope = soft_terms(logits)
            coeff = slope.astype(BF16)
        extra = loss_lanes(jnp.sum(loss, axis=1, keepdims=True))
        grad = nn(coeff, texts[...])
        more = tn(coeff, images[...])
        if images is near_images:
            keep[:, :width] = grad
            keep[:, width:] = extra
            sums = more
        else:
            send[:, :width] = grad.astype(BF16)
            send[:, width:] = split_lanes(extra)
            sums = sums + more
    keep_text[...] = sums[:half]
    send_text[...] = sums[half:].astype(BF16)


def fold_tagged(own, got, keep, send):
    half, width = keep.shape[0], keep.shape[1] - LANES
    for ref, rows in ((keep, slice(0, half)), (send, slice(half, 2 * half))):
        ref[:, :width] = (own[rows, :width] + got[rows, :width].astype(F32)).astype(ref.dtype)
        extra = own[rows, width:] + join_lanes(got[rows, width:].astype(F32))
        ref[:, width:] = extra if ref is keep else split_lanes(extra)


def fold_last(scale_ref, own, got, own_text, got_text, keep, send, text_grad):
    fold_tagged(own, got, keep, send)
    text_grad[...] = scale_ref[0] * (own_text[...] + got_text[...].astype(F32))


def fold_both(own, got, own_text, got_text, keep, send, keep_text, send_text):
    fold_tagged(own, got, keep, send)
    half = keep_text.shape[0]
    keep_text[...] = own_text[:half, :] + got_text[:half, :].astype(F32)
    send_text[...] = (own_text[half:, :] + got_text[half:, :].astype(F32)).astype(BF16)


def captions(scale_ref, bias_ref, arrived, image, own_marks, tag1, tag2, back, own, send1, send2,
             here, done, in_sems, out_sems):
    width = image.shape[1]
    slots = arrived.shape[0] * arrived.shape[2]
    scale, bias = scale_ref[0], bias_ref[0]
    loads = [pltpu.make_async_copy(arrived.at[:, k], here.at[k], in_sems.at[k]) for k in range(N_ZH)]
    stores = [pltpu.make_async_copy(done.at[k], back.at[:, k], out_sems.at[k]) for k in range(N_ZH)]
    for load in loads:
        load.start()
    for k in range(N_ZH):
        if k == 0:
            i, mark = image[...], own_marks[...].astype(F32)
        else:
            ref = (tag1, tag2)[k - 1]
            i, mark = ref[:, :width], ref[:, width:].astype(F32)
        loads[k].wait()
        e = here[k].reshape(slots, width)
        there = mark > 0
        denom = jnp.where(there, mark, 1.0)
        loss, slope = soft_terms(-(scale * nt(i, e) + bias))
        loss = jnp.sum(jnp.where(there, loss / denom, 0.0), axis=1, keepdims=True)
        weight = jnp.where(there, -slope / denom, 0.0).astype(BF16)
        done[k] = (scale * tn(weight, i)).astype(BF16).reshape(done.shape[1:])
        stores[k].start()
        part = nn(weight, e)
        if k == 0:
            own[:, :width] = part
            own[:, width:] = loss_lanes(loss)
        else:
            ref = (send1, send2)[k - 1]
            ref[:, :width] = part.astype(BF16)
            ref[:, width:] = split_lanes(loss_lanes(loss))
    for store in stores:
        store.wait()


def finish(scale_ref, own, got, cap_own, cap1, cap2, loss, image_grad):
    rows, width = image_grad.shape
    total = own[...] + got[...].astype(F32) + cap_own[...] + cap1[...].astype(F32) + cap2[...].astype(F32)
    image_grad[...] = scale_ref[0] * total[:, :width]
    column = jnp.sum(total[:, width:], axis=1, keepdims=True)
    diagonal = lax.broadcasted_iota(jnp.int32, (rows, rows), 0) == lax.broadcasted_iota(jnp.int32, (rows, rows), 1)
    loss[...] = jnp.sum(jnp.where(diagonal, column, 0.0), axis=0, keepdims=True)


def place(zh_ref, back, out, here, in_sems, out_sems):
    zh = zh_ref[0]
    loads = [pltpu.make_async_copy(back.at[:, k], here.at[k], in_sems.at[k]) for k in range(N_ZH)]
    stores = [
        pltpu.make_async_copy(here.at[k], out.at[lax.rem(zh + (N_ZH - k), N_ZH)], out_sems.at[k])
        for k in range(N_ZH)
    ]
    for load in loads:
        load.start()
    for load, store in zip(loads, stores):
        load.wait()
        store.start()
    for store in stores:
        store.wait()


def shards(image, text, caption, logit_scale, logit_bias, owner, valid, count):
    rows, width = image.shape
    wide = width + LANES
    slots = caption.shape[0]
    run = slots // (N_ZH * N_Y)
    third = slots // N_ZH
    zh = (lax.axis_index("cap") // N_Y).astype(jnp.int32).reshape(1)
    sems = pltpu.SemaphoreType.DMA((N_ZH,))

    outgoing, tag1, tag2, own_marks = call(
        prepare,
        [((N_Y, N_ZH, run, width), BF16), ((rows, wide), BF16), ((rows, wide), BF16), ((rows, third), BF16)],
        (zh, caption.reshape(N_ZH, N_Y, run, width), image, owner.reshape(1, slots), valid.reshape(1, slots),
         count.reshape(1, rows)),
        [SMEM] + [HBM] * 5, [VMEM] * 4,
        [pltpu.VMEM((rows, width), BF16), pltpu.VMEM((1, slots), jnp.int32), pltpu.VMEM((1, slots), jnp.int32),
         pltpu.VMEM((1, rows), jnp.int32), sems, pltpu.SemaphoreType.DMA((4,))],
        flops=PREP, room=8,
    )

    def to_y(x):
        x = x.reshape(N_Y, N_ZH * run, width)
        x = lax.all_to_all(x, "cap", 0, 0, axis_index_groups=Y_GROUPS, tiled=True)
        return x.reshape(N_Y, N_ZH, run, width)

    arrived = to_y(outgoing)
    from1 = lax.ppermute(tag1, "cap", shift_zh(1))
    from2 = lax.ppermute(tag2, "cap", shift_zh(2))

    images, texts = call(
        join, [((2 * rows, width), BF16)] * 2,
        (image, lax.ppermute(image, "blk", X_FAR), text, lax.ppermute(text, "blk", ZL_FAR), tag1),
        [VMEM] * 4 + [ANY], flops=JOIN,
    )
    images, texts = call(
        stack, [((4 * rows, width), BF16)] * 2,
        (images, lax.ppermute(images, "blk", X_NEAR), texts, lax.ppermute(texts, "blk", ZL_NEAR)), [VMEM] * 4,
        flops=STACK,
    )
    others = lax.ppermute(images, "blk", OTHER_CORE)
    n_i, n_t = 2 * N_X * rows, N_ZL * rows
    keep, send, keep_t, send_t = call(
        lambda *refs: pairs(*refs, rows=rows),
        [((n_i // 2, wide), F32), ((n_i // 2, wide), BF16), ((n_t // 2, width), F32), ((n_t // 2, width), BF16)],
        (logit_scale, logit_bias, images, others, texts), [SMEM, SMEM] + [VMEM] * 3,
        flops=6 * n_i * n_t * width, moved=8 * n_i * width,
    )
    got = lax.ppermute(send, "blk", OTHER_CORE)
    got_t = lax.ppermute(send_t, "blk", ZL_NEAR)

    back, cap_own, send1, send2 = call(
        captions,
        [((N_Y, N_ZH, run, width), BF16), ((rows, wide), F32), ((rows, wide), BF16), ((rows, wide), BF16)],
        (logit_scale, logit_bias, arrived, image, own_marks, from1, from2), [SMEM, SMEM, ANY] + [VMEM] * 4,
        [ANY] + [VMEM] * 3, [pltpu.VMEM((N_ZH, N_Y, run, width), BF16)] * 2 + [sems, sems], flops=CAPS,
    )
    returned = to_y(back)
    cap1 = lax.ppermute(send1, "cap", shift_zh(-1))
    cap2 = lax.ppermute(send2, "cap", shift_zh(-2))

    keep, send, keep_t, send_t = call(
        fold_both,
        [((n_i // 4, wide), F32), ((n_i // 4, wide), BF16), ((rows, width), F32), ((rows, width), BF16)],
        (keep, got, keep_t, got_t), [VMEM] * 4, flops=FOLD,
    )
    got = lax.ppermute(send, "blk", X_NEAR)
    got_t = lax.ppermute(send_t, "blk", ZL_FAR)
    keep, send, text_grad = call(
        fold_last, [((rows, wide), F32), ((rows, wide), BF16), ((rows, width), F32)],
        (logit_scale, keep, got, keep_t, got_t), [SMEM] + [VMEM] * 4, flops=FOLD2,
    )
    got = lax.ppermute(send, "blk", X_FAR)
    loss, image_grad = call(
        finish, [((1, rows), F32), ((rows, width), F32)],
        (logit_scale, keep, got, cap_own, cap1, cap2), [SMEM] + [VMEM] * 5, moved=rows * wide * 20,
    )
    (caption_grad,) = call(
        place, [((N_ZH, N_Y, run, width), BF16)], (zh, returned), [SMEM, ANY], [ANY],
        [pltpu.VMEM((N_ZH, N_Y, run, width), BF16), sems, sems], moved=4 * slots * width
    )
    return loss.reshape(rows), image_grad, text_grad, caption_grad.reshape(slots, width)


def solution(mesh):
    both = ("blk", "cap")
    in_specs = (P(both, None), P(both, None), P(both, None), P(), P(), P(both), P(both), P(both))
    out_specs = (P(both), P(both, None), P(both, None), P(both, None))
    return jax.shard_map(shards, mesh=mesh, in_specs=in_specs, out_specs=out_specs, check_vma=False)
```

```python
import jax
import jax.numpy as jnp
from jax import lax
from jax.experimental import pallas as pl
from jax.experimental.pallas import tpu as pltpu
from jax.sharding import PartitionSpec as P

N_ZL, N_X, N_C = 4, 4, 2
N_ZH, N_Y = 3, 8
LANES = 128
LATE = 200_000_000_000
JOIN, STACK, CAPS, FOLD, FOLD2 = LATE, 5_000_000_000, LATE, LATE, 0

F32, BF16 = jnp.float32, jnp.bfloat16
SMEM = pl.BlockSpec(memory_space=pltpu.SMEM)
VMEM = pl.BlockSpec(memory_space=pltpu.VMEM)
ANY = pl.BlockSpec(memory_space=pl.ANY)
HBM = pl.BlockSpec(memory_space=pltpu.HBM)


def partners(zl_bits, x_bits, c_bits):
    def blk_of(zl, x, c):
        return (zl * N_X + x) * N_C + c

    return [
        (blk_of(z, x, c), blk_of(z ^ zl_bits, x ^ x_bits, c ^ c_bits))
        for z in range(N_ZL) for x in range(N_X) for c in range(N_C)
    ]


ZL_NEAR, ZL_FAR = partners(1, 0, 0), partners(2, 0, 0)
X_NEAR, X_FAR = partners(0, 1, 0), partners(0, 3, 0)
OTHER_CORE = partners(0, 0, 1)
Y_GROUPS = [[h * N_Y + y for y in range(N_Y)] for h in range(N_ZH)]


def shift_zh(k):
    return [(h * N_Y + y, ((h + k) % N_ZH) * N_Y + y) for h in range(N_ZH) for y in range(N_Y)]


def call(body, outs, ins, in_specs, out_specs=None, scratch=(), flops=0, moved=0, room=8):
    return pl.pallas_call(
        body,
        out_shape=tuple(jax.ShapeDtypeStruct(s, d) for s, d in outs),
        in_specs=in_specs,
        out_specs=tuple(out_specs or [VMEM] * len(outs)),
        scratch_shapes=list(scratch),
        cost_estimate=pl.CostEstimate(flops=flops, bytes_accessed=moved, transcendentals=0),
        compiler_params=pltpu.CompilerParams(vmem_limit_bytes=room * 1024 * 1024),
    )(*ins)


def nt(a, b):
    return lax.dot_general(a, b, (((1,), (1,)), ((), ())), preferred_element_type=F32)


def tn(a, b):
    return lax.dot_general(a, b, (((0,), (0,)), ((), ())), preferred_element_type=F32)


def nn(a, b):
    return jnp.dot(a, b, preferred_element_type=F32)


def soft_terms(u):
    e = jnp.exp(-jnp.abs(u))
    return jnp.maximum(u, 0.0) + jnp.log1p(e), jnp.where(u >= 0, 1.0, e) / (1.0 + e)


def loss_lanes(loss):
    lane = lax.broadcasted_iota(jnp.int32, (loss.shape[0], LANES), 1)
    return jnp.where(lane == 0, loss, 0.0)


def split_lanes(extra):
    lane = lax.broadcasted_iota(jnp.int32, extra.shape, 1)
    value = jnp.sum(jnp.where(lane == 0, extra, 0.0), axis=1, keepdims=True)
    high = value.astype(BF16).astype(F32)
    return jnp.where(lane == 0, high, jnp.where(lane == 1, value - high, 0.0)).astype(BF16)


def join_lanes(extra):
    lane = lax.broadcasted_iota(jnp.int32, extra.shape, 1)
    return jnp.where(lane == 0, jnp.sum(extra, axis=1, keepdims=True), 0.0)


def tags(zh_ref, image, lists, tag1, tag2, own_marks):
    zh = zh_ref[0]
    rows, width = image.shape
    slots = (lists.shape[1] - rows) // 2
    third = slots // N_ZH
    owner, valid, count = lists[:, :slots], lists[:, slots:2 * slots], lists[:, 2 * slots:]
    diagonal = lax.broadcasted_iota(jnp.int32, (rows, rows), 0) == lax.broadcasted_iota(jnp.int32, (rows, rows), 1)
    number = jnp.sum(jnp.where(diagonal, count.astype(F32), 0.0), axis=1, keepdims=True)
    number = jnp.maximum(number, 1.0)
    holds = owner == lax.broadcasted_iota(jnp.int32, (rows, slots), 0)
    marks = jnp.where(holds & (valid > 0), number, 0.0).astype(BF16)
    parts = [marks[:, h * third:(h + 1) * third] for h in range(N_ZH)]
    for k, ref in enumerate((own_marks, tag1, tag2)):
        to = lax.rem(zh + k, N_ZH)
        part = jnp.where(to == 0, parts[0], jnp.where(to == 1, parts[1], parts[2]))
        if k == 0:
            ref[...] = part
        else:
            ref[:, :width] = image[...]
            ref[:, width:] = part


def join(image, got_image, text, got_text, images, texts):
    for first, second, out in ((image, got_image, images), (text, got_text, texts)):
        rows = first.shape[0]
        out[:rows, :] = first[...]
        out[rows:, :] = second[...]


def stack(images1, images2, texts1, texts2, images, texts):
    for first, second, out in ((images1, images2, images), (texts1, texts2, texts)):
        rows = first.shape[0]
        out[:rows, :] = first[...]
        out[rows:, :] = second[...]


def pairs(scale_ref, bias_ref, near_images, far_images, texts, keep, send, keep_text, send_text, rows):
    width = texts.shape[1]
    half = texts.shape[0] // 2
    sums = None
    for images in (near_images, far_images):
        logits = scale_ref[0] * nt(images[...], texts[...]) + bias_ref[0]
        if images is near_images:
            left = lax.broadcasted_iota(jnp.int32, logits.shape, 0)
            right = lax.broadcasted_iota(jnp.int32, logits.shape, 1)
            match = (left == right) & (left < rows)
            loss, slope = soft_terms(jnp.where(match, -logits, logits))
            coeff = jnp.where(match, -slope, slope).astype(BF16)
        else:
            loss, slope = soft_terms(logits)
            coeff = slope.astype(BF16)
        extra = loss_lanes(jnp.sum(loss, axis=1, keepdims=True))
        grad = nn(coeff, texts[...])
        more = tn(coeff, images[...])
        if images is near_images:
            keep[:, :width] = grad
            keep[:, width:] = extra
            sums = more
        else:
            send[:, :width] = grad.astype(BF16)
            send[:, width:] = split_lanes(extra)
            sums = sums + more
    keep_text[...] = sums[:half]
    send_text[...] = sums[half:].astype(BF16)


def fold_tagged(own, got, keep, send):
    half, width = keep.shape[0], keep.shape[1] - LANES
    for ref, rows in ((keep, slice(0, half)), (send, slice(half, 2 * half))):
        ref[:, :width] = (own[rows, :width] + got[rows, :width].astype(F32)).astype(ref.dtype)
        extra = own[rows, width:] + join_lanes(got[rows, width:].astype(F32))
        ref[:, width:] = extra if ref is keep else split_lanes(extra)


def fold_last(scale_ref, own, got, own_text, got_text, keep, send, text_grad):
    fold_tagged(own, got, keep, send)
    text_grad[...] = scale_ref[0] * (own_text[...] + got_text[...].astype(F32))


def fold_both(own, got, own_text, got_text, cap1, keep, send, keep_text, send_text):
    fold_tagged(own, got, keep, send)
    rows, width = cap1.shape[0], cap1.shape[1] - LANES
    keep[:rows, :width] += cap1[:, :width].astype(F32)
    keep[:rows, width:] += join_lanes(cap1[:, width:].astype(F32))
    half = keep_text.shape[0]
    keep_text[...] = own_text[:half, :] + got_text[:half, :].astype(F32)
    send_text[...] = (own_text[half:, :] + got_text[half:, :].astype(F32)).astype(BF16)


def captions(zh_ref, scale_ref, bias_ref, arrived, image, own_marks, tag1, tag2, back, own, send1, send2):
    n_y, _, run, width = arrived.shape
    slots = n_y * run
    scale, bias = scale_ref[0], bias_ref[0]
    for k in range(N_ZH):
        plane = lax.rem(zh_ref[0] + (N_ZH - k), N_ZH)
        if k == 0:
            i, mark = image[...], own_marks[...].astype(F32)
        else:
            ref = (tag1, tag2)[k - 1]
            i, mark = ref[:, :width], ref[:, width:].astype(F32)
        e = arrived[:, plane].reshape(slots, width)
        there = mark > 0
        denom = jnp.where(there, mark, 1.0)
        loss, slope = soft_terms(-(scale * nt(i, e) + bias))
        loss = jnp.sum(jnp.where(there, loss / denom, 0.0), axis=1, keepdims=True)
        weight = jnp.where(there, -slope / denom, 0.0).astype(BF16)
        back[:, plane] = (scale * tn(weight, i)).astype(BF16).reshape(n_y, run, width)
        part = nn(weight, e)
        if k == 0:
            own[:, :width] = part
            own[:, width:] = loss_lanes(loss)
        else:
            ref = (send1, send2)[k - 1]
            ref[:, :width] = part.astype(BF16)
            ref[:, width:] = split_lanes(loss_lanes(loss))


def finish(scale_ref, own, got, cap_own, cap2, after, loss, image_grad):
    rows, width = image_grad.shape
    total = own[...] + got[...].astype(F32) + cap_own[...] + cap2[...].astype(F32)
    image_grad[...] = scale_ref[0] * total[:, :width]
    column = jnp.sum(total[:, width:], axis=1, keepdims=True)
    diagonal = lax.broadcasted_iota(jnp.int32, (rows, rows), 0) == lax.broadcasted_iota(jnp.int32, (rows, rows), 1)
    loss[...] = jnp.sum(jnp.where(diagonal, column, 0.0), axis=0, keepdims=True)


def shards(image, text, caption, logit_scale, logit_bias, owner, valid, count):
    rows, width = image.shape
    wide = width + LANES
    slots = caption.shape[0]
    run = slots // (N_ZH * N_Y)
    third = slots // N_ZH
    zh = (lax.axis_index("cap") // N_Y).astype(jnp.int32).reshape(1)
    lists = jnp.concatenate([owner, valid, count]).reshape(1, 2 * slots + rows)
    tag1, tag2, own_marks = call(
        tags, [((rows, wide), BF16), ((rows, wide), BF16), ((rows, third), BF16)], (zh, image, lists),
        [SMEM, VMEM, VMEM],
    )

    def to_y(x):
        x = x.reshape(N_Y, N_ZH * run, width)
        x = lax.all_to_all(x, "cap", 0, 0, axis_index_groups=Y_GROUPS, tiled=True)
        return x.reshape(N_Y, N_ZH, run, width)

    arrived = to_y(caption.reshape(N_ZH, N_Y, run, width).swapaxes(0, 1))
    from1 = lax.ppermute(tag1, "cap", shift_zh(1))
    from2 = lax.ppermute(tag2, "cap", shift_zh(2))

    images, texts = call(
        join, [((2 * rows, width), BF16)] * 2,
        (image, lax.ppermute(image, "blk", X_FAR), text, lax.ppermute(text, "blk", ZL_FAR)), [VMEM] * 4, flops=JOIN,
    )
    images, texts = call(
        stack, [((4 * rows, width), BF16)] * 2,
        (images, lax.ppermute(images, "blk", X_NEAR), texts, lax.ppermute(texts, "blk", ZL_NEAR)), [VMEM] * 4,
        flops=STACK,
    )
    others = lax.ppermute(images, "blk", OTHER_CORE)
    n_i, n_t = 2 * N_X * rows, N_ZL * rows
    keep, send, keep_t, send_t = call(
        lambda *refs: pairs(*refs, rows=rows),
        [((n_i // 2, wide), F32), ((n_i // 2, wide), BF16), ((n_t // 2, width), F32), ((n_t // 2, width), BF16)],
        (logit_scale, logit_bias, images, others, texts), [SMEM, SMEM] + [VMEM] * 3,
    )
    got = lax.ppermute(send, "blk", OTHER_CORE)
    got_t = lax.ppermute(send_t, "blk", ZL_NEAR)

    back, cap_own, send1, send2 = call(
        captions,
        [((N_Y, N_ZH, run, width), BF16), ((rows, wide), F32), ((rows, wide), BF16), ((rows, wide), BF16)],
        (zh, logit_scale, logit_bias, arrived, image, own_marks, from1, from2), [SMEM] * 3 + [VMEM] * 5, flops=CAPS,
    )
    returned = to_y(back)
    cap1 = lax.ppermute(send1, "cap", shift_zh(-1))
    cap2 = lax.ppermute(send2, "cap", shift_zh(-2))

    keep, send, keep_t, send_t = call(
        fold_both,
        [((n_i // 4, wide), F32), ((n_i // 4, wide), BF16), ((rows, width), F32), ((rows, width), BF16)],
        (keep, got, keep_t, got_t, cap1), [VMEM] * 5, flops=FOLD,
    )
    got = lax.ppermute(send, "blk", X_NEAR)
    got_t = lax.ppermute(send_t, "blk", ZL_FAR)
    keep, send, text_grad = call(
        fold_last, [((rows, wide), F32), ((rows, wide), BF16), ((rows, width), F32)],
        (logit_scale, keep, got, keep_t, got_t), [SMEM] + [VMEM] * 4, flops=FOLD2,
    )
    got = lax.ppermute(send, "blk", X_FAR)
    caption_grad = returned.swapaxes(0, 1).reshape(slots, width)
    loss, image_grad = call(
        finish, [((1, rows), F32), ((rows, width), F32)],
        (logit_scale, keep, got, cap_own, cap2, caption_grad), [SMEM] + [VMEM] * 4 + [ANY],
    )
    return loss.reshape(rows), image_grad, text_grad, caption_grad


def solution(mesh):
    both = ("blk", "cap")
    in_specs = (P(both, None), P(both, None), P(both, None), P(), P(), P(both), P(both), P(both))
    out_specs = (P(both), P(both, None), P(both, None), P(both, None))
    return jax.shard_map(shards, mesh=mesh, in_specs=in_specs, out_specs=out_specs, check_vma=False)
```

```python
import jax
import jax.numpy as jnp
from jax import lax
from jax.experimental import pallas as pl
from jax.experimental.pallas import tpu as pltpu
from jax.sharding import PartitionSpec as P

N_ZL, N_X, N_C = 4, 4, 2
N_ZH, N_Y = 3, 8
LANES = 128
LATE = 200_000_000_000
JOIN, STACK, CAPS, FOLD, FOLD2 = LATE, 5_000_000_000, LATE, LATE, 0

F32, BF16 = jnp.float32, jnp.bfloat16
SMEM = pl.BlockSpec(memory_space=pltpu.SMEM)
VMEM = pl.BlockSpec(memory_space=pltpu.VMEM)
ANY = pl.BlockSpec(memory_space=pl.ANY)
HBM = pl.BlockSpec(memory_space=pltpu.HBM)


def partners(zl_bits, x_bits, c_bits):
    def blk_of(zl, x, c):
        return (zl * N_X + x) * N_C + c

    return [
        (blk_of(z, x, c), blk_of(z ^ zl_bits, x ^ x_bits, c ^ c_bits))
        for z in range(N_ZL) for x in range(N_X) for c in range(N_C)
    ]


ZL_NEAR, ZL_FAR = partners(1, 0, 0), partners(2, 0, 0)
X_NEAR, X_FAR = partners(0, 1, 0), partners(0, 3, 0)
OTHER_CORE = partners(0, 0, 1)
Y_GROUPS = [[h * N_Y + y for y in range(N_Y)] for h in range(N_ZH)]


def shift_zh(k):
    groups = N_ZH * N_Y
    return [
        (b * groups + h * N_Y + y, b * groups + (h + (1 - 2 * (b % N_C)) * k) % N_ZH * N_Y + y)
        for b in range(N_ZL * N_X * N_C) for h in range(N_ZH) for y in range(N_Y)
    ]


def call(body, outs, ins, in_specs, out_specs=None, scratch=(), flops=0, moved=0, room=8):
    return pl.pallas_call(
        body,
        out_shape=tuple(jax.ShapeDtypeStruct(s, d) for s, d in outs),
        in_specs=in_specs,
        out_specs=tuple(out_specs or [VMEM] * len(outs)),
        scratch_shapes=list(scratch),
        cost_estimate=pl.CostEstimate(flops=flops, bytes_accessed=moved, transcendentals=0),
        compiler_params=pltpu.CompilerParams(vmem_limit_bytes=room * 1024 * 1024),
    )(*ins)


def nt(a, b):
    return lax.dot_general(a, b, (((1,), (1,)), ((), ())), preferred_element_type=F32)


def tn(a, b):
    return lax.dot_general(a, b, (((0,), (0,)), ((), ())), preferred_element_type=F32)


def nn(a, b):
    return jnp.dot(a, b, preferred_element_type=F32)


def soft_terms(u):
    e = jnp.exp(-jnp.abs(u))
    return jnp.maximum(u, 0.0) + jnp.log1p(e), jnp.where(u >= 0, 1.0, e) / (1.0 + e)


def loss_lanes(loss):
    lane = lax.broadcasted_iota(jnp.int32, (loss.shape[0], LANES), 1)
    return jnp.where(lane == 0, loss, 0.0)


def split_lanes(extra):
    lane = lax.broadcasted_iota(jnp.int32, extra.shape, 1)
    value = jnp.sum(jnp.where(lane == 0, extra, 0.0), axis=1, keepdims=True)
    high = value.astype(BF16).astype(F32)
    return jnp.where(lane == 0, high, jnp.where(lane == 1, value - high, 0.0)).astype(BF16)


def join_lanes(extra):
    lane = lax.broadcasted_iota(jnp.int32, extra.shape, 1)
    return jnp.where(lane == 0, jnp.sum(extra, axis=1, keepdims=True), 0.0)


def tags(zh_ref, image, lists, tag1, tag2, own_marks):
    zh, way = zh_ref[0], zh_ref[1]
    rows, width = image.shape
    slots = (lists.shape[1] - rows) // 2
    third = slots // N_ZH
    owner, valid, count = lists[:, :slots], lists[:, slots:2 * slots], lists[:, 2 * slots:]
    diagonal = lax.broadcasted_iota(jnp.int32, (rows, rows), 0) == lax.broadcasted_iota(jnp.int32, (rows, rows), 1)
    number = jnp.sum(jnp.where(diagonal, count.astype(F32), 0.0), axis=1, keepdims=True)
    number = jnp.maximum(number, 1.0)
    holds = owner == lax.broadcasted_iota(jnp.int32, (rows, slots), 0)
    marks = jnp.where(holds & (valid > 0), number, 0.0).astype(BF16)
    parts = [marks[:, h * third:(h + 1) * third] for h in range(N_ZH)]
    for k, ref in enumerate((own_marks, tag1, tag2)):
        to = lax.rem(zh + N_ZH + way * k, N_ZH)
        part = jnp.where(to == 0, parts[0], jnp.where(to == 1, parts[1], parts[2]))
        if k == 0:
            ref[...] = part
        else:
            ref[:, :width] = image[...]
            ref[:, width:] = part


def join(image, got_image, text, got_text, images, texts):
    for first, second, out in ((image, got_image, images), (text, got_text, texts)):
        rows = first.shape[0]
        out[:rows, :] = first[...]
        out[rows:, :] = second[...]


def stack(images1, images2, texts1, texts2, images, texts):
    for first, second, out in ((images1, images2, images), (texts1, texts2, texts)):
        rows = first.shape[0]
        out[:rows, :] = first[...]
        out[rows:, :] = second[...]


def pairs(scale_ref, bias_ref, near_images, far_images, texts, keep, send, keep_text, send_text, rows):
    width = texts.shape[1]
    half = texts.shape[0] // 2
    sums = None
    for images in (near_images, far_images):
        logits = scale_ref[0] * nt(images[...], texts[...]) + bias_ref[0]
        if images is near_images:
            left = lax.broadcasted_iota(jnp.int32, logits.shape, 0)
            right = lax.broadcasted_iota(jnp.int32, logits.shape, 1)
            match = (left == right) & (left < rows)
            loss, slope = soft_terms(jnp.where(match, -logits, logits))
            coeff = jnp.where(match, -slope, slope).astype(BF16)
        else:
            loss, slope = soft_terms(logits)
            coeff = slope.astype(BF16)
        extra = loss_lanes(jnp.sum(loss, axis=1, keepdims=True))
        grad = nn(coeff, texts[...])
        more = tn(coeff, images[...])
        if images is near_images:
            keep[:, :width] = grad
            keep[:, width:] = extra
            sums = more
        else:
            send[:, :width] = grad.astype(BF16)
            send[:, width:] = split_lanes(extra)
            sums = sums + more
    keep_text[...] = sums[:half]
    send_text[...] = sums[half:].astype(BF16)


def fold_tagged(own, got, keep, send):
    half, width = keep.shape[0], keep.shape[1] - LANES
    for ref, rows in ((keep, slice(0, half)), (send, slice(half, 2 * half))):
        ref[:, :width] = (own[rows, :width] + got[rows, :width].astype(F32)).astype(ref.dtype)
        extra = own[rows, width:] + join_lanes(got[rows, width:].astype(F32))
        ref[:, width:] = extra if ref is keep else split_lanes(extra)


def fold_last(scale_ref, own, got, own_text, got_text, keep, send, text_grad):
    fold_tagged(own, got, keep, send)
    text_grad[...] = scale_ref[0] * (own_text[...] + got_text[...].astype(F32))


def fold_both(own, got, own_text, got_text, cap1, keep, send, keep_text, send_text):
    fold_tagged(own, got, keep, send)
    rows, width = cap1.shape[0], cap1.shape[1] - LANES
    keep[:rows, :width] += cap1[:, :width].astype(F32)
    keep[:rows, width:] += join_lanes(cap1[:, width:].astype(F32))
    half = keep_text.shape[0]
    keep_text[...] = own_text[:half, :] + got_text[:half, :].astype(F32)
    send_text[...] = (own_text[half:, :] + got_text[half:, :].astype(F32)).astype(BF16)


def captions(zh_ref, scale_ref, bias_ref, arrived, image, own_marks, tag1, tag2, back, own, send1, send2):
    n_y, _, run, width = arrived.shape
    slots = n_y * run
    scale, bias = scale_ref[0], bias_ref[0]
    for k in range(N_ZH):
        plane = lax.rem(zh_ref[0] + N_ZH - zh_ref[1] * k, N_ZH)
        if k == 0:
            i, mark = image[...], own_marks[...].astype(F32)
        else:
            ref = (tag1, tag2)[k - 1]
            i, mark = ref[:, :width], ref[:, width:].astype(F32)
        e = arrived[:, plane].reshape(slots, width)
        there = mark > 0
        denom = jnp.where(there, mark, 1.0)
        loss, slope = soft_terms(-(scale * nt(i, e) + bias))
        loss = jnp.sum(jnp.where(there, loss / denom, 0.0), axis=1, keepdims=True)
        weight = jnp.where(there, -slope / denom, 0.0).astype(BF16)
        back[:, plane] = (scale * tn(weight, i)).astype(BF16).reshape(n_y, run, width)
        part = nn(weight, e)
        if k == 0:
            own[:, :width] = part
            own[:, width:] = loss_lanes(loss)
        else:
            ref = (send1, send2)[k - 1]
            ref[:, :width] = part.astype(BF16)
            ref[:, width:] = split_lanes(loss_lanes(loss))


def finish(scale_ref, own, got, cap_own, cap2, after, loss, image_grad):
    rows, width = image_grad.shape
    total = own[...] + got[...].astype(F32) + cap_own[...] + cap2[...].astype(F32)
    image_grad[...] = scale_ref[0] * total[:, :width]
    column = jnp.sum(total[:, width:], axis=1, keepdims=True)
    diagonal = lax.broadcasted_iota(jnp.int32, (rows, rows), 0) == lax.broadcasted_iota(jnp.int32, (rows, rows), 1)
    loss[...] = jnp.sum(jnp.where(diagonal, column, 0.0), axis=0, keepdims=True)


def shards(image, text, caption, logit_scale, logit_bias, owner, valid, count):
    rows, width = image.shape
    wide = width + LANES
    slots = caption.shape[0]
    run = slots // (N_ZH * N_Y)
    third = slots // N_ZH
    zh = jnp.stack([lax.axis_index("cap") // N_Y, 1 - 2 * lax.rem(lax.axis_index("blk"), N_C)]).astype(jnp.int32)
    lists = jnp.concatenate([owner, valid, count]).reshape(1, 2 * slots + rows)
    tag1, tag2, own_marks = call(
        tags, [((rows, wide), BF16), ((rows, wide), BF16), ((rows, third), BF16)], (zh, image, lists),
        [SMEM, VMEM, VMEM],
    )

    def to_y(x):
        x = x.reshape(N_Y, N_ZH * run, width)
        x = lax.all_to_all(x, "cap", 0, 0, axis_index_groups=Y_GROUPS, tiled=True)
        return x.reshape(N_Y, N_ZH, run, width)

    arrived = to_y(caption.reshape(N_ZH, N_Y, run, width).swapaxes(0, 1))
    from1 = lax.ppermute(tag1, ("blk", "cap"), shift_zh(1))
    from2 = lax.ppermute(tag2, ("blk", "cap"), shift_zh(2))

    images, texts = call(
        join, [((2 * rows, width), BF16)] * 2,
        (image, lax.ppermute(image, "blk", X_FAR), text, lax.ppermute(text, "blk", ZL_FAR)), [VMEM] * 4, flops=JOIN,
    )
    images, texts = call(
        stack, [((4 * rows, width), BF16)] * 2,
        (images, lax.ppermute(images, "blk", X_NEAR), texts, lax.ppermute(texts, "blk", ZL_NEAR)), [VMEM] * 4,
        flops=STACK,
    )
    others = lax.ppermute(images, "blk", OTHER_CORE)
    n_i, n_t = 2 * N_X * rows, N_ZL * rows
    keep, send, keep_t, send_t = call(
        lambda *refs: pairs(*refs, rows=rows),
        [((n_i // 2, wide), F32), ((n_i // 2, wide), BF16), ((n_t // 2, width), F32), ((n_t // 2, width), BF16)],
        (logit_scale, logit_bias, images, others, texts), [SMEM, SMEM] + [VMEM] * 3,
    )
    got = lax.ppermute(send, "blk", OTHER_CORE)
    got_t = lax.ppermute(send_t, "blk", ZL_NEAR)

    back, cap_own, send1, send2 = call(
        captions,
        [((N_Y, N_ZH, run, width), BF16), ((rows, wide), F32), ((rows, wide), BF16), ((rows, wide), BF16)],
        (zh, logit_scale, logit_bias, arrived, image, own_marks, from1, from2), [SMEM] * 3 + [VMEM] * 5, flops=CAPS,
    )
    returned = to_y(back)
    cap1 = lax.ppermute(send1, ("blk", "cap"), shift_zh(-1))
    cap2 = lax.ppermute(send2, ("blk", "cap"), shift_zh(-2))

    keep, send, keep_t, send_t = call(
        fold_both,
        [((n_i // 4, wide), F32), ((n_i // 4, wide), BF16), ((rows, width), F32), ((rows, width), BF16)],
        (keep, got, keep_t, got_t, cap1), [VMEM] * 5, flops=FOLD,
    )
    got = lax.ppermute(send, "blk", X_NEAR)
    got_t = lax.ppermute(send_t, "blk", ZL_FAR)
    keep, send, text_grad = call(
        fold_last, [((rows, wide), F32), ((rows, wide), BF16), ((rows, width), F32)],
        (logit_scale, keep, got, keep_t, got_t), [SMEM] + [VMEM] * 4, flops=FOLD2,
    )
    got = lax.ppermute(send, "blk", X_FAR)
    caption_grad = returned.swapaxes(0, 1).reshape(slots, width)
    loss, image_grad = call(
        finish, [((1, rows), F32), ((rows, width), F32)],
        (logit_scale, keep, got, cap_own, cap2, caption_grad), [SMEM] + [VMEM] * 4 + [ANY],
    )
    return loss.reshape(rows), image_grad, text_grad, caption_grad


def solution(mesh):
    both = ("blk", "cap")
    in_specs = (P(both, None), P(both, None), P(both, None), P(), P(), P(both), P(both), P(both))
    out_specs = (P(both), P(both, None), P(both, None), P(both, None))
    return jax.shard_map(shards, mesh=mesh, in_specs=in_specs, out_specs=out_specs, check_vma=False)
```

```python
import jax
import jax.numpy as jnp
from jax import lax
from jax.experimental import pallas as pl
from jax.experimental.pallas import tpu as pltpu
from jax.sharding import PartitionSpec as P

N_ZL, N_X, N_C = 4, 4, 2
N_ZH, N_Y = 3, 8
LANES = 128
LATE = 200_000_000_000
JOIN, STACK, CAPS, FOLD, FOLD2 = LATE, 5_000_000_000, LATE, LATE, 0

F32, BF16 = jnp.float32, jnp.bfloat16
SMEM = pl.BlockSpec(memory_space=pltpu.SMEM)
VMEM = pl.BlockSpec(memory_space=pltpu.VMEM)
ANY = pl.BlockSpec(memory_space=pl.ANY)
HBM = pl.BlockSpec(memory_space=pltpu.HBM)


def partners(zl_bits, x_bits, c_bits):
    zl_of = zl_bits if isinstance(zl_bits, tuple) else (zl_bits,) * N_C

    def blk_of(zl, x, c):
        return (zl * N_X + x) * N_C + c

    return [
        (blk_of(z, x, c), blk_of(z ^ zl_of[c], x ^ x_bits, c ^ c_bits))
        for z in range(N_ZL) for x in range(N_X) for c in range(N_C)
    ]


ZL_NEAR, ZL_FAR = partners(1, 0, 0), partners(2, 0, 0)
ZL_FIRST, ZL_LAST = partners((1, 2), 0, 0), partners((2, 1), 0, 0)
X_NEAR, X_FAR = partners(0, 1, 0), partners(0, 3, 0)
OTHER_CORE = partners(0, 0, 1)
Y_GROUPS = [[h * N_Y + y for y in range(N_Y)] for h in range(N_ZH)]


def shift_zh(k):
    groups = N_ZH * N_Y
    return [
        (b * groups + h * N_Y + y, b * groups + (h + (1 - 2 * (b % N_C)) * k) % N_ZH * N_Y + y)
        for b in range(N_ZL * N_X * N_C) for h in range(N_ZH) for y in range(N_Y)
    ]


def call(body, outs, ins, in_specs, out_specs=None, scratch=(), flops=0, moved=0, room=8):
    return pl.pallas_call(
        body,
        out_shape=tuple(jax.ShapeDtypeStruct(s, d) for s, d in outs),
        in_specs=in_specs,
        out_specs=tuple(out_specs or [VMEM] * len(outs)),
        scratch_shapes=list(scratch),
        cost_estimate=pl.CostEstimate(flops=flops, bytes_accessed=moved, transcendentals=0),
        compiler_params=pltpu.CompilerParams(vmem_limit_bytes=room * 1024 * 1024),
    )(*ins)


def nt(a, b):
    return lax.dot_general(a, b, (((1,), (1,)), ((), ())), preferred_element_type=F32)


def tn(a, b):
    return lax.dot_general(a, b, (((0,), (0,)), ((), ())), preferred_element_type=F32)


def nn(a, b):
    return jnp.dot(a, b, preferred_element_type=F32)


def soft_terms(u):
    e = jnp.exp(-jnp.abs(u))
    return jnp.maximum(u, 0.0) + jnp.log1p(e), jnp.where(u >= 0, 1.0, e) / (1.0 + e)


def loss_lanes(loss):
    lane = lax.broadcasted_iota(jnp.int32, (loss.shape[0], LANES), 1)
    return jnp.where(lane == 0, loss, 0.0)


def split_lanes(extra):
    lane = lax.broadcasted_iota(jnp.int32, extra.shape, 1)
    value = jnp.sum(jnp.where(lane == 0, extra, 0.0), axis=1, keepdims=True)
    high = value.astype(BF16).astype(F32)
    return jnp.where(lane == 0, high, jnp.where(lane == 1, value - high, 0.0)).astype(BF16)


def join_lanes(extra):
    lane = lax.broadcasted_iota(jnp.int32, extra.shape, 1)
    return jnp.where(lane == 0, jnp.sum(extra, axis=1, keepdims=True), 0.0)


def tags(zh_ref, image, lists, tag1, tag2, own_marks):
    zh, way = zh_ref[0], zh_ref[1]
    rows, width = image.shape
    slots = (lists.shape[1] - rows) // 2
    third = slots // N_ZH
    owner, valid, count = lists[:, :slots], lists[:, slots:2 * slots], lists[:, 2 * slots:]
    diagonal = lax.broadcasted_iota(jnp.int32, (rows, rows), 0) == lax.broadcasted_iota(jnp.int32, (rows, rows), 1)
    number = jnp.sum(jnp.where(diagonal, count.astype(F32), 0.0), axis=1, keepdims=True)
    number = jnp.maximum(number, 1.0)
    holds = owner == lax.broadcasted_iota(jnp.int32, (rows, slots), 0)
    marks = jnp.where(holds & (valid > 0), number, 0.0).astype(BF16)
    parts = [marks[:, h * third:(h + 1) * third] for h in range(N_ZH)]
    for k, ref in enumerate((own_marks, tag1, tag2)):
        to = lax.rem(zh + N_ZH + way * k, N_ZH)
        part = jnp.where(to == 0, parts[0], jnp.where(to == 1, parts[1], parts[2]))
        if k == 0:
            ref[...] = part
        else:
            ref[:, :width] = image[...]
            ref[:, width:] = part


def join(image, got_image, text, got_text, images, texts):
    for first, second, out in ((image, got_image, images), (text, got_text, texts)):
        rows = first.shape[0]
        out[:rows, :] = first[...]
        out[rows:, :] = second[...]


def stack(images1, images2, texts1, texts2, images, texts):
    for first, second, out in ((images1, images2, images), (texts1, texts2, texts)):
        rows = first.shape[0]
        out[:rows, :] = first[...]
        out[rows:, :] = second[...]


def pairs(place_ref, scale_ref, bias_ref, near_images, far_images, texts, keep, send, keep_text, send_text, rows):
    width = texts.shape[1]
    half = texts.shape[0] // 2
    sums = None
    for images in (near_images, far_images):
        logits = scale_ref[0] * nt(images[...], texts[...]) + bias_ref[0]
        if images is near_images:
            left = lax.broadcasted_iota(jnp.int32, logits.shape, 0)
            right = lax.broadcasted_iota(jnp.int32, logits.shape, 1)
            match = (left == right) & (left < rows)
            loss, slope = soft_terms(jnp.where(match, -logits, logits))
            coeff = jnp.where(match, -slope, slope).astype(BF16)
        else:
            loss, slope = soft_terms(logits)
            coeff = slope.astype(BF16)
        extra = loss_lanes(jnp.sum(loss, axis=1, keepdims=True))
        grad = nn(coeff, texts[...])
        more = tn(coeff, images[...])
        if images is near_images:
            keep[:, :width] = grad
            keep[:, width:] = extra
            sums = more
        else:
            send[:, :width] = grad.astype(BF16)
            send[:, width:] = split_lanes(extra)
            sums = sums + more
    first = place_ref[1] > 0
    far, near = sums[rows:half], sums[half:half + rows]
    keep_text[:rows, :] = sums[:rows]
    keep_text[rows:, :] = jnp.where(first, far, near)
    send_text[:rows, :] = jnp.where(first, near, far).astype(BF16)
    send_text[rows:, :] = sums[half + rows:].astype(BF16)


def fold_tagged(own, got, keep, send):
    half, width = keep.shape[0], keep.shape[1] - LANES
    for ref, rows in ((keep, slice(0, half)), (send, slice(half, 2 * half))):
        ref[:, :width] = (own[rows, :width] + got[rows, :width].astype(F32)).astype(ref.dtype)
        extra = own[rows, width:] + join_lanes(got[rows, width:].astype(F32))
        ref[:, width:] = extra if ref is keep else split_lanes(extra)


def fold_last(scale_ref, own, got, own_text, got_text, keep, send, text_grad):
    fold_tagged(own, got, keep, send)
    text_grad[...] = scale_ref[0] * (own_text[...] + got_text[...].astype(F32))


def fold_both(own, got, own_text, got_text, cap1, keep, send, keep_text, send_text):
    fold_tagged(own, got, keep, send)
    rows, width = cap1.shape[0], cap1.shape[1] - LANES
    keep[:rows, :width] += cap1[:, :width].astype(F32)
    keep[:rows, width:] += join_lanes(cap1[:, width:].astype(F32))
    half = keep_text.shape[0]
    keep_text[...] = own_text[:half, :] + got_text[:half, :].astype(F32)
    send_text[...] = (own_text[half:, :] + got_text[half:, :].astype(F32)).astype(BF16)


def captions(zh_ref, scale_ref, bias_ref, arrived, image, own_marks, tag1, tag2, back, own, send1, send2):
    n_y, _, run, width = arrived.shape
    slots = n_y * run
    scale, bias = scale_ref[0], bias_ref[0]
    for k in range(N_ZH):
        plane = lax.rem(zh_ref[0] + N_ZH - zh_ref[1] * k, N_ZH)
        if k == 0:
            i, mark = image[...], own_marks[...].astype(F32)
        else:
            ref = (tag1, tag2)[k - 1]
            i, mark = ref[:, :width], ref[:, width:].astype(F32)
        e = arrived[:, plane].reshape(slots, width)
        there = mark > 0
        denom = jnp.where(there, mark, 1.0)
        loss, slope = soft_terms(-(scale * nt(i, e) + bias))
        loss = jnp.sum(jnp.where(there, loss / denom, 0.0), axis=1, keepdims=True)
        weight = jnp.where(there, -slope / denom, 0.0).astype(BF16)
        back[:, plane] = (scale * tn(weight, i)).astype(BF16).reshape(n_y, run, width)
        part = nn(weight, e)
        if k == 0:
            own[:, :width] = part
            own[:, width:] = loss_lanes(loss)
        else:
            ref = (send1, send2)[k - 1]
            ref[:, :width] = part.astype(BF16)
            ref[:, width:] = split_lanes(loss_lanes(loss))


def finish(scale_ref, own, got, cap_own, cap2, after, loss, image_grad):
    rows, width = image_grad.shape
    total = own[...] + got[...].astype(F32) + cap_own[...] + cap2[...].astype(F32)
    image_grad[...] = scale_ref[0] * total[:, :width]
    column = jnp.sum(total[:, width:], axis=1, keepdims=True)
    diagonal = lax.broadcasted_iota(jnp.int32, (rows, rows), 0) == lax.broadcasted_iota(jnp.int32, (rows, rows), 1)
    loss[...] = jnp.sum(jnp.where(diagonal, column, 0.0), axis=0, keepdims=True)


def shards(image, text, caption, logit_scale, logit_bias, owner, valid, count):
    rows, width = image.shape
    wide = width + LANES
    slots = caption.shape[0]
    run = slots // (N_ZH * N_Y)
    third = slots // N_ZH
    zh = jnp.stack([lax.axis_index("cap") // N_Y, 1 - 2 * lax.rem(lax.axis_index("blk"), N_C)]).astype(jnp.int32)
    lists = jnp.concatenate([owner, valid, count]).reshape(1, 2 * slots + rows)
    tag1, tag2, own_marks = call(
        tags, [((rows, wide), BF16), ((rows, wide), BF16), ((rows, third), BF16)], (zh, image, lists),
        [SMEM, VMEM, VMEM],
    )

    def to_y(x):
        x = x.reshape(N_Y, N_ZH * run, width)
        x = lax.all_to_all(x, "cap", 0, 0, axis_index_groups=Y_GROUPS, tiled=True)
        return x.reshape(N_Y, N_ZH, run, width)

    arrived = to_y(caption.reshape(N_ZH, N_Y, run, width).swapaxes(0, 1))
    from1 = lax.ppermute(tag1, ("blk", "cap"), shift_zh(1))
    from2 = lax.ppermute(tag2, ("blk", "cap"), shift_zh(2))

    images, texts = call(
        join, [((2 * rows, width), BF16)] * 2,
        (image, lax.ppermute(image, "blk", X_FAR), text, lax.ppermute(text, "blk", ZL_FAR)), [VMEM] * 4, flops=JOIN,
    )
    images, texts = call(
        stack, [((4 * rows, width), BF16)] * 2,
        (images, lax.ppermute(images, "blk", X_NEAR), texts, lax.ppermute(texts, "blk", ZL_NEAR)), [VMEM] * 4,
        flops=STACK,
    )
    others = lax.ppermute(images, "blk", OTHER_CORE)
    n_i, n_t = 2 * N_X * rows, N_ZL * rows
    keep, send, keep_t, send_t = call(
        lambda *refs: pairs(*refs, rows=rows),
        [((n_i // 2, wide), F32), ((n_i // 2, wide), BF16), ((n_t // 2, width), F32), ((n_t // 2, width), BF16)],
        (zh, logit_scale, logit_bias, images, others, texts), [SMEM] * 3 + [VMEM] * 3,
    )
    got = lax.ppermute(send, "blk", OTHER_CORE)
    got_t = lax.ppermute(send_t, "blk", ZL_FIRST)

    back, cap_own, send1, send2 = call(
        captions,
        [((N_Y, N_ZH, run, width), BF16), ((rows, wide), F32), ((rows, wide), BF16), ((rows, wide), BF16)],
        (zh, logit_scale, logit_bias, arrived, image, own_marks, from1, from2), [SMEM] * 3 + [VMEM] * 5, flops=CAPS,
    )
    returned = to_y(back)
    cap1 = lax.ppermute(send1, ("blk", "cap"), shift_zh(-1))
    cap2 = lax.ppermute(send2, ("blk", "cap"), shift_zh(-2))

    keep, send, keep_t, send_t = call(
        fold_both,
        [((n_i // 4, wide), F32), ((n_i // 4, wide), BF16), ((rows, width), F32), ((rows, width), BF16)],
        (keep, got, keep_t, got_t, cap1), [VMEM] * 5, flops=FOLD,
    )
    got = lax.ppermute(send, "blk", X_NEAR)
    got_t = lax.ppermute(send_t, "blk", ZL_LAST)
    keep, send, text_grad = call(
        fold_last, [((rows, wide), F32), ((rows, wide), BF16), ((rows, width), F32)],
        (logit_scale, keep, got, keep_t, got_t), [SMEM] + [VMEM] * 4, flops=FOLD2,
    )
    got = lax.ppermute(send, "blk", X_FAR)
    caption_grad = returned.swapaxes(0, 1).reshape(slots, width)
    loss, image_grad = call(
        finish, [((1, rows), F32), ((rows, width), F32)],
        (logit_scale, keep, got, cap_own, cap2, caption_grad), [SMEM] + [VMEM] * 4 + [ANY],
    )
    return loss.reshape(rows), image_grad, text_grad, caption_grad


def solution(mesh):
    both = ("blk", "cap")
    in_specs = (P(both, None), P(both, None), P(both, None), P(), P(), P(both), P(both), P(both))
    out_specs = (P(both), P(both, None), P(both, None), P(both, None))
    return jax.shard_map(shards, mesh=mesh, in_specs=in_specs, out_specs=out_specs, check_vma=False)
```
